512 devices in a mesh: group: 8 (over y, core), dev: 64 (over x, z).
Axes of the slice: x: 4, y: 4, z: 16, core: 2. Of those that a mesh axis runs over, the one named last changes fastest.
Arguments:
- bin_index: int32 [2097152, 128], P(('group', 'dev')), may hold values from 0 to 63
- gradient: bfloat16 [2097152], P(('group', 'dev')), may hold values from -6 to 6
- hessian: bfloat16 [2097152], P(('group', 'dev')), may hold values from 0.049804688 to 0.25
- child_id: int32 [2097152], P(('group', 'dev')), may hold values from 0 to 63
- smaller_side: int32 [32], replicated, may hold values from 0 to 1
Outputs:
- best_gain: float32 [32, 128], P('group', 'dev')
- child_best: float32 [32], P('group')
The draws below stay inside these ranges and needn't reach their ends.
All inputs are finite; a program needn't handle non-finite values.
Results may differ from the reference program's by a relative error of at most 0.0003.
Values sent between devices are 32-bit elements; how exact they have to be, the bound alone decides.
No kernel may reach another device: no remote copies, remote signals or barrier semaphores. Data moves between devices by JAX's collectives and lax.ppermute only.
A program may use at most 64 MiB of HBM per device.

```python
import math
import jax
import jax.numpy as jnp
from jax import lax

FEAT = 128
BINS = 64
PAIRS = 32
ROWS = 2097152


def place_ends(values, own_key, least, largest):
    spot = [jax.random.randint(jax.random.fold_in(own_key, axis), (), 0, length) for axis, length in enumerate(values.shape)]
    main_axis = values.shape.index(max(values.shape))
    beside = spot[:main_axis] + [(spot[main_axis] + 1) % values.shape[main_axis]] + spot[main_axis + 1:]
    return values.at[tuple(spot)].set(least).at[tuple(beside)].set(largest)


def shard_levels(own_key, extent, cuts, low, top_value):
    loudness = 1.0
    for position, parts in cuts:
        draws = jax.random.uniform(jax.random.fold_in(jax.random.fold_in(own_key, 6), position), (parts,), jnp.float32, low / len(cuts), top_value / len(cuts))
        loudness = loudness * jnp.repeat(jnp.exp(draws), extent[position] // parts).reshape((-1,) + (1,) * (len(extent) - 1 - position))
    return loudness


def gaussian(own_key, extent, deviation, reach, cuts=(), kind=jnp.bfloat16):
    result = deviation * jax.random.normal(own_key, extent, jnp.float32)
    if cuts:
        result = result * shard_levels(own_key, extent, cuts, -0.22, 0.18)
    return jnp.clip(result, -reach, reach).astype(kind)


def setup_inputs(seed: int = 0) -> dict:
    key_list = jax.random.split(jax.random.key(seed), 6)
    return {
        "bin_index": place_ends(jax.random.randint(key_list[0], (ROWS, FEAT), 0, BINS), jax.random.fold_in(key_list[0], 1), 0, BINS - 1).astype(jnp.int32),
        "gradient": gaussian(key_list[1], (ROWS,), 1.0, 6.0, ((0, 512),)),
        "hessian": jnp.clip(0.049804688 + 0.20019531 * jax.random.uniform(key_list[2], (ROWS,), jnp.float32) ** shard_levels(key_list[2], (ROWS,), ((0, 512),), -0.2, 0.2), 0.049804688, 0.25).astype(jnp.bfloat16),
        "child_id": place_ends(jax.random.randint(key_list[3], (ROWS,), 0, 2 * PAIRS), jax.random.fold_in(key_list[3], 1), 0, (2 * PAIRS) - 1).astype(jnp.int32),
        "smaller_side": place_ends(jax.random.randint(key_list[4], (PAIRS,), 0, 2), jax.random.fold_in(key_list[4], 1), 0, 1).astype(jnp.int32),
    }


reg_lambda = 1.0


def split_gains(hist_grad, hist_hess):
    left_grad = jnp.cumsum(hist_grad, axis=-1)[..., :-1]
    left_hess = jnp.cumsum(hist_hess, axis=-1)[..., :-1]
    total_grad = jnp.sum(hist_grad, axis=-1, keepdims=True)
    total_hess = jnp.sum(hist_hess, axis=-1, keepdims=True)
    right_grad = total_grad - left_grad
    value = left_grad * left_grad / (left_hess + reg_lambda)
    value = value + right_grad * right_grad / (total_hess - left_hess + reg_lambda)
    value = value - total_grad * total_grad / (total_hess + reg_lambda)
    return jnp.max(value, axis=-1)


def reference(bin_index, gradient, hessian, child_id, smaller_side):
    row_count = bin_index.shape[0]
    pair_index = (child_id // 2).astype(jnp.int32)
    member = (child_id - 2 * pair_index == smaller_side[pair_index]).astype(jnp.float32)
    values = jnp.stack([gradient.astype(jnp.float32) * member, hessian.astype(jnp.float32) * member], axis=1)
    block_size = math.gcd(FEAT, 8)
    offsets = jnp.arange(block_size, dtype=jnp.int32) * (PAIRS * BINS)
    base_index = (pair_index * BINS).astype(jnp.int32)

    def one_block(number):
        columns = lax.dynamic_slice_in_dim(bin_index, (number * block_size).astype(jnp.int32), block_size, 1)
        segment = base_index[:, None] + columns + offsets[None, :]
        spread = jnp.broadcast_to(values[:, None, :], (row_count, block_size, 2))
        summed = jax.ops.segment_sum(spread.reshape(-1, 2), segment.reshape(-1).astype(jnp.int32), num_segments=block_size * PAIRS * BINS)
        return summed.reshape(block_size, PAIRS, BINS, 2)

    hist = lax.map(one_block, jnp.arange(FEAT // block_size, dtype=jnp.int32)).reshape(FEAT, PAIRS, BINS, 2)
    best_gain = split_gains(hist[..., 0], hist[..., 1]).T
    child_best = jnp.max(best_gain, axis=1)
    return best_gain, child_best
```

```python
import functools

import jax
import jax.numpy as jnp
from jax import lax
from jax.experimental import pallas as pl
from jax.experimental.pallas import tpu as pltpu
from jax.sharding import Mesh
from jax.sharding import PartitionSpec as P

BINS = 64
LANES = 128
AXES = ("y", "core", "x", "z")
reg_lambda = 1.0


def hist_kernel(block, together, bin_ref, grad_ref, hess_ref, child_ref, target_ref,
                keep_ref, send_ref, turned, weights):
    rows, features = bin_ref.shape
    blocks = rows // block
    wide = block // LANES
    columns = target_ref.shape[0]
    is_grad = lax.broadcasted_iota(jnp.int32, (8, block), 0) < 4
    for k in range(blocks):
        turned[k] = bin_ref[k * block : (k + 1) * block, :].astype(jnp.float32).T
        parts = range(k * wide, (k + 1) * wide)
        child = jnp.concatenate([child_ref[i : i + 1, :] for i in parts], axis=1)
        grad = jnp.concatenate([grad_ref[i : i + 1, :] for i in parts], axis=1)
        hess = jnp.concatenate([hess_ref[i : i + 1, :] for i in parts], axis=1)
        value = jnp.where(is_grad, grad, hess)
        chosen = [
            child == jnp.concatenate([target_ref[8 * n : 8 * n + 8, :]] * wide, axis=1)
            for n in range(columns // 8)
        ]
        weights[k] = jnp.concatenate(
            [jnp.where(c, value, 0.0) for c in chosen], axis=0
        ).astype(jnp.bfloat16)

    level = lax.broadcasted_iota(jnp.int32, (16, block), 0).astype(jnp.float32)
    levels = [(level + 16.0 * n).astype(jnp.bfloat16) for n in range(BINS // 16)]
    one = jnp.ones((16, block), jnp.bfloat16)
    zero = jnp.zeros((16, block), jnp.bfloat16)

    def some_features(group, carry):
        total = jnp.zeros((columns, together * BINS), jnp.float32)
        for k in range(blocks):
            upto = []
            for i in range(together):
                row = turned[k, pl.ds(group * together + i, 1), :]
                row = jnp.broadcast_to(row, (16, block)).astype(jnp.bfloat16)
                upto += [jnp.where(row <= level, one, zero) for level in levels]
            total = total + lax.dot_general(
                weights[k], jnp.concatenate(upto, axis=0), (((1,), (1,)), ((), ())),
                preferred_element_type=jnp.float32,
            )
        for pair in range(together * BINS // LANES):
            owner = group * (together * BINS // LANES) + pair
            for n in range(columns // 8):
                piece = total[8 * n : 8 * n + 8, pair * LANES : (pair + 1) * LANES]
                out = keep_ref if n < columns // 16 else send_ref
                out[n % (columns // 16), owner] = piece
        return carry

    lax.fori_loop(0, features // together, some_features, 0)


def histograms(bin_index, gradient, hessian, child_id, target, block=512, together=8):
    rows, features = bin_index.shape
    columns = target.shape[0]
    half = jax.ShapeDtypeStruct((columns // 16, features * BINS // LANES, 8, LANES), jnp.float32)
    vmem = pl.BlockSpec(memory_space=pltpu.VMEM)
    return pl.pallas_call(
        functools.partial(hist_kernel, block, together),
        out_shape=(half, half),
        in_specs=[vmem] * 5,
        out_specs=(vmem, vmem),
        scratch_shapes=[
            pltpu.VMEM((rows // block, features, block), jnp.float32),
            pltpu.VMEM((rows // block, columns, block), jnp.bfloat16),
        ],
        compiler_params=pltpu.CompilerParams(vmem_limit_bytes=48 * 2**20),
        name="histograms",
    )(bin_index, gradient, hessian, child_id, target)


def gain_kernel(pieces_ref, best_ref, told_ref):
    left = jnp.sum(pieces_ref[...], axis=0)
    lane = lax.broadcasted_iota(jnp.int32, (8, LANES), 1)
    first = jnp.sum(jnp.where(lane == BINS - 1, left, 0.0), axis=1, keepdims=True)
    second = jnp.sum(jnp.where(lane == 2 * BINS - 1, left, 0.0), axis=1, keepdims=True)
    total = jnp.where(lane < BINS, first, second)
    left_grad, left_hess = left[:4], left[4:]
    total_grad, total_hess = total[:4], total[4:]
    right_grad = total_grad - left_grad
    value = left_grad * left_grad / (left_hess + reg_lambda)
    value = value + right_grad * right_grad / (total_hess - left_hess + reg_lambda)
    value = value - total_grad * total_grad / (total_hess + reg_lambda)
    lane = lane[:4]
    bottom = jnp.float32(-jnp.inf)
    inner = lane % BINS < BINS - 1
    one = jnp.max(jnp.where(inner & (lane < BINS), value, bottom), axis=1, keepdims=True)
    two = jnp.max(jnp.where(inner & (lane >= BINS), value, bottom), axis=1, keepdims=True)
    best_ref[...] = jnp.concatenate([one, two], axis=1)
    diagonal = lane == lax.broadcasted_iota(jnp.int32, (4, LANES), 0)
    told = jnp.sum(jnp.where(diagonal, jnp.maximum(one, two), 0.0), axis=0, keepdims=True)
    told_ref[...] = jnp.broadcast_to(told, told_ref.shape)


def gains(pieces, listeners):
    vmem = pl.BlockSpec(memory_space=pltpu.VMEM)
    return pl.pallas_call(
        gain_kernel,
        out_shape=(
            jax.ShapeDtypeStruct((4, 2), jnp.float32),
            jax.ShapeDtypeStruct((listeners, LANES), jnp.float32),
        ),
        in_specs=[vmem],
        out_specs=(vmem, vmem),
        name="gains",
    )(pieces)


def body(bin_index, gradient, hessian, child_id, smaller_side):
    ny, nc, nx, nz = (lax.axis_size(a) for a in AXES)
    rows = bin_index.shape[0]
    mine = lax.axis_index("core")
    leaves = 2 * jnp.arange(smaller_side.shape[0], dtype=jnp.int32) + smaller_side
    leaves = leaves.reshape(ny, nc, 4)
    ordered = jnp.stack(
        [
            jnp.where(mine == 0, leaves[:, 0], leaves[:, 1]),
            jnp.where(mine == 0, leaves[:, 1], leaves[:, 0]),
        ]
    )
    target = jnp.broadcast_to(ordered[:, :, None, :, None], (nc, ny, 2, 4, LANES))
    target = target.reshape(-1, LANES)
    keep, send = histograms(
        bin_index,
        gradient.astype(jnp.float32).reshape(rows // LANES, LANES),
        hessian.astype(jnp.float32).reshape(rows // LANES, LANES),
        child_id.reshape(rows // LANES, LANES),
        target,
    )
    chip = keep + lax.ppermute(send, "core", [(0, 1), (1, 0)])
    chip = chip.reshape(ny * nx, nz, 8, LANES)
    plane = jnp.sum(lax.all_to_all(chip, ("y", "x"), 0, 0, tiled=True), axis=0)
    pieces = lax.all_to_all(plane, "z", 0, 0, tiled=True)
    best_gain, told = gains(pieces, nx * nz)
    heard = lax.all_to_all(told, ("x", "z"), 0, 0, tiled=True)
    child_best = jnp.max(heard, axis=0)[:4]
    return best_gain, child_best


def solution(mesh):
    split = Mesh(mesh.devices.reshape(4, 2, 4, 16), AXES)
    every = P(AXES)
    return jax.shard_map(
        body,
        mesh=split,
        in_specs=(P(AXES, None), every, every, every, P()),
        out_specs=(P(("y", "core"), ("x", "z")), P(("y", "core"))),
        check_vma=False,
    )
```

```python
import functools

import jax
import jax.numpy as jnp
from jax import lax
from jax.experimental import pallas as pl
from jax.experimental.pallas import tpu as pltpu
from jax.sharding import Mesh
from jax.sharding import PartitionSpec as P

BINS = 64
LANES = 128
AXES = ("y", "core", "x", "z")
reg_lambda = 1.0


def hist_kernel(block, together, side_hbm, bin_ref, grad_hbm, hess_hbm, child_hbm,
                keep_ref, send_ref, side_ref, grad_ref, hess_ref, child_ref, arrived, packed, copied):
    rows, features = bin_ref.shape
    leaves = side_ref.shape[0]
    blocks = rows // block
    wide = block // LANES
    bins = pltpu.make_async_copy(bin_ref, arrived, copied.at[4])
    small = [
        pltpu.make_async_copy(source, target, copied.at[i])
        for i, (source, target) in enumerate(
            [(side_hbm, side_ref), (child_hbm, child_ref), (grad_hbm, grad_ref), (hess_hbm, hess_ref)]
        )
    ]
    for copy in small + [bins]:
        copy.start()
    keep_ref[...] = jnp.zeros_like(keep_ref)
    send_ref[...] = jnp.zeros_like(send_ref)

    for copy in small:
        copy.wait()
    mine = lax.axis_index("core")
    child = child_ref[...]
    code = jnp.zeros(child.shape, jnp.int32)
    for leaf in range(leaves):
        y, core, low = leaf // 8, leaf // 4 % 2, leaf % 4
        place = (core ^ mine) * (leaves // 2) + y * 4 + low
        code = jnp.where(child == 2 * leaf + side_ref[leaf], place + 1, code)
    code = code.astype(jnp.float32)
    member = jnp.where(code > 0.0, 1.0, 0.0)

    lane = [lax.broadcasted_iota(jnp.int32, (LANES, LANES), d) for d in (0, 1)]
    before = jnp.where(lane[0] < lane[1], 1.0, 0.0).astype(jnp.bfloat16)
    lines = child.shape[0]
    line = [lax.broadcasted_iota(jnp.int32, (lines, lines), d) for d in (0, 1)]
    above = jnp.where(line[1] < line[0], 1.0, 0.0).astype(jnp.bfloat16)
    short = member.astype(jnp.bfloat16)
    rank = jnp.dot(short, before, preferred_element_type=jnp.float32)
    count = jnp.dot(short, jnp.ones((LANES, LANES), jnp.bfloat16), preferred_element_type=jnp.float32)
    base = jnp.dot(above, count.astype(jnp.bfloat16), preferred_element_type=jnp.float32)
    dest = jnp.where(code > 0.0, rank + base, -2.0 * rows)
    grad = grad_ref[...].astype(jnp.float32)
    hess = hess_ref[...].astype(jnp.float32)

    level = lax.broadcasted_iota(jnp.int32, (16, block), 0).astype(jnp.float32)
    slots = [(level + 16.0 * n).astype(jnp.bfloat16) for n in range(block // 16)]
    one = jnp.ones((16, block), jnp.bfloat16)
    zero = jnp.zeros((16, block), jnp.bfloat16)

    def wide_row(array, s):
        return jnp.concatenate([array[i : i + 1, :] for i in range(s * wide, (s + 1) * wide)], axis=1)

    fill = jnp.zeros((13, block), jnp.float32)
    counts = [jnp.sum(member[s * wide : (s + 1) * wide, :]).astype(jnp.int32) for s in range(blocks)]
    done = [jnp.int32(0)]
    for n in counts:
        done.append(done[-1] + n)
    current = jnp.zeros((features + 16, block), jnp.float32)
    bins.wait()
    for s in range(blocks):
        first, last = (lax.div(n, block) for n in done[s : s + 2])
        values = jnp.concatenate(
            [
                arrived[s * block : (s + 1) * block, :].astype(jnp.float32).T,
                wide_row(code, s), wide_row(grad, s), wide_row(hess, s), fill,
            ],
            axis=0,
        ).astype(jnp.bfloat16)
        slot = wide_row(dest, s) - (first * block).astype(jnp.float32)
        moved = []
        for half in range(2):
            near = jnp.broadcast_to(slot - float(half * block), (16, block)).astype(jnp.bfloat16)
            moved += [jnp.where(near == n, one, zero) for n in slots]
        placed = lax.dot_general(
            values, jnp.concatenate(moved, axis=0), (((1,), (1,)), ((), ())),
            preferred_element_type=jnp.float32,
        )
        current = current + placed[:, :block]
        packed[first] = current
        current = jnp.where(last > first, placed[:, block:], current)
    packed[lax.div(done[-1], block)] = current

    sub = lax.broadcasted_iota(jnp.int32, (8, block), 0)
    is_grad = sub < 4
    place = (sub % 4 + 1).astype(jnp.float32)
    levels = slots[: BINS // 16]

    def one_block(k, carry):
        value = jnp.where(is_grad, packed[k, features + 1 : features + 2, :], packed[k, features + 2 : features + 3, :])
        owned = packed[k, features : features + 1, :] - place
        weights = jnp.concatenate(
            [jnp.where(owned == float(4 * n), value, 0.0) for n in range(leaves // 4)], axis=0
        ).astype(jnp.bfloat16)
        for group in range(features // together):
            upto = []
            for f in range(group * together, (group + 1) * together):
                row = jnp.broadcast_to(packed[k, f : f + 1, :], (16, block)).astype(jnp.bfloat16)
                upto += [jnp.where(row <= n, one, zero) for n in levels]
            part = lax.dot_general(
                weights, jnp.concatenate(upto, axis=0), (((1,), (1,)), ((), ())),
                preferred_element_type=jnp.float32,
            )
            for pair in range(together * BINS // LANES):
                owner = group * (together * BINS // LANES) + pair
                for n in range(leaves // 4):
                    out = keep_ref if n < leaves // 8 else send_ref
                    out[n % (leaves // 8), owner] += part[8 * n : 8 * n + 8, pair * LANES : (pair + 1) * LANES]
        return carry

    lax.fori_loop(0, lax.div(done[-1] + (block - 1), block), one_block, 0)


def histograms(bin_index, gradient, hessian, child_id, smaller_side, block=256, together=4):
    rows, features = bin_index.shape
    leaves = smaller_side.shape[0]
    lines = (rows // LANES, LANES)
    half = jax.ShapeDtypeStruct((leaves // 8, features * BINS // LANES, 8, LANES), jnp.float32)
    vmem = pl.BlockSpec(memory_space=pltpu.VMEM)
    return pl.pallas_call(
        functools.partial(hist_kernel, block, together),
        out_shape=(half, half),
        in_specs=[pl.BlockSpec(memory_space=pltpu.HBM)] * 5,
        out_specs=(vmem, vmem),
        scratch_shapes=[
            pltpu.SMEM((leaves,), jnp.int32),
            pltpu.VMEM(lines, jnp.bfloat16),
            pltpu.VMEM(lines, jnp.bfloat16),
            pltpu.VMEM(lines, jnp.int32),
            pltpu.VMEM((rows, features), jnp.int32),
            pltpu.VMEM((rows // block + 1, features + 16, block), jnp.float32),
            pltpu.SemaphoreType.DMA((5,)),
        ],
        compiler_params=pltpu.CompilerParams(vmem_limit_bytes=60 * 2**20),
        name="histograms",
    )(smaller_side, bin_index, gradient.reshape(lines), hessian.reshape(lines), child_id.reshape(lines))


def gain_kernel(pieces_ref, best_ref, told_ref):
    left = jnp.sum(pieces_ref[...], axis=0)
    lane = lax.broadcasted_iota(jnp.int32, (8, LANES), 1)
    first = jnp.sum(jnp.where(lane == BINS - 1, left, 0.0), axis=1, keepdims=True)
    second = jnp.sum(jnp.where(lane == 2 * BINS - 1, left, 0.0), axis=1, keepdims=True)
    total = jnp.where(lane < BINS, first, second)
    left_grad, left_hess = left[:4], left[4:]
    total_grad, total_hess = total[:4], total[4:]
    right_grad = total_grad - left_grad
    value = left_grad * left_grad / (left_hess + reg_lambda)
    value = value + right_grad * right_grad / (total_hess - left_hess + reg_lambda)
    value = value - total_grad * total_grad / (total_hess + reg_lambda)
    lane = lane[:4]
    bottom = jnp.float32(-jnp.inf)
    inner = lane % BINS < BINS - 1
    one = jnp.max(jnp.where(inner & (lane < BINS), value, bottom), axis=1, keepdims=True)
    two = jnp.max(jnp.where(inner & (lane >= BINS), value, bottom), axis=1, keepdims=True)
    best_ref[...] = jnp.concatenate([one, two], axis=1)
    diagonal = lane == lax.broadcasted_iota(jnp.int32, (4, LANES), 0)
    told = jnp.sum(jnp.where(diagonal, jnp.maximum(one, two), 0.0), axis=0, keepdims=True)
    told_ref[...] = jnp.broadcast_to(told, told_ref.shape)


def gains(pieces, listeners):
    vmem = pl.BlockSpec(memory_space=pltpu.VMEM)
    return pl.pallas_call(
        gain_kernel,
        out_shape=(
            jax.ShapeDtypeStruct((4, 2), jnp.float32),
            jax.ShapeDtypeStruct((listeners, LANES), jnp.float32),
        ),
        in_specs=[vmem],
        out_specs=(vmem, vmem),
        compiler_params=pltpu.CompilerParams(vmem_limit_bytes=4 * 2**20),
        name="gains",
    )(pieces)


def body(bin_index, gradient, hessian, child_id, smaller_side):
    ny, nc, nx, nz = (lax.axis_size(a) for a in AXES)
    keep, send = histograms(bin_index, gradient, hessian, child_id, smaller_side)
    chip = keep + lax.ppermute(send, "core", [(0, 1), (1, 0)])
    chip = chip.reshape(ny * nx, nz, 8, LANES)
    plane = jnp.sum(lax.all_to_all(chip, ("y", "x"), 0, 0, tiled=True), axis=0)
    pieces = lax.all_to_all(plane, "z", 0, 0, tiled=True)
    best_gain, told = gains(pieces, nx * nz)
    heard = lax.all_to_all(told, ("x", "z"), 0, 0, tiled=True)
    child_best = jnp.max(heard, axis=0)[:4]
    return best_gain, child_best


def solution(mesh):
    split = Mesh(mesh.devices.reshape(4, 2, 4, 16), AXES)
    every = P(AXES)
    return jax.shard_map(
        body,
        mesh=split,
        in_specs=(P(AXES, None), every, every, every, P()),
        out_specs=(P(("y", "core"), ("x", "z")), P(("y", "core"))),
        check_vma=False,
    )
```

```python
import functools

import jax
import jax.numpy as jnp
from jax import lax
from jax.experimental import pallas as pl
from jax.experimental.pallas import tpu as pltpu
from jax.sharding import Mesh
from jax.sharding import PartitionSpec as P

BINS = 64
LANES = 128
AXES = ("y", "core", "x", "z")
reg_lambda = 1.0


def hist_kernel(block, joined, together, side_hbm, bin_ref, grad_hbm, hess_hbm, child_hbm,
                keep_ref, send_ref, side_ref, grad_ref, hess_ref, child_ref, arrived, packed, copied):
    rows, features = bin_ref.shape
    leaves = side_ref.shape[0]
    blocks = rows // block
    wide = block // LANES
    bins = pltpu.make_async_copy(bin_ref, arrived, copied.at[4])
    small = [
        pltpu.make_async_copy(source, target, copied.at[i])
        for i, (source, target) in enumerate(
            [(side_hbm, side_ref), (child_hbm, child_ref), (grad_hbm, grad_ref), (hess_hbm, hess_ref)]
        )
    ]
    for copy in small + [bins]:
        copy.start()
    keep_ref[...] = jnp.zeros_like(keep_ref)
    send_ref[...] = jnp.zeros_like(send_ref)

    for copy in small:
        copy.wait()
    mine = lax.axis_index("core")
    child = child_ref[...]
    code = jnp.zeros(child.shape, jnp.int32)
    for leaf in range(leaves):
        y, core, low = leaf // 8, leaf // 4 % 2, leaf % 4
        place = (core ^ mine) * (leaves // 2) + y * 4 + low
        code = jnp.where(child == 2 * leaf + side_ref[leaf], place + 1, code)
    code = code.astype(jnp.float32)
    member = jnp.where(code > 0.0, 1.0, 0.0)

    lane = [lax.broadcasted_iota(jnp.int32, (LANES, LANES), d) for d in (0, 1)]
    before = jnp.where(lane[0] < lane[1], 1.0, 0.0).astype(jnp.bfloat16)
    lines = child.shape[0]
    line = [lax.broadcasted_iota(jnp.int32, (lines, lines), d) for d in (0, 1)]
    above = jnp.where(line[1] < line[0], 1.0, 0.0).astype(jnp.bfloat16)
    short = member.astype(jnp.bfloat16)
    rank = jnp.dot(short, before, preferred_element_type=jnp.float32)
    count = jnp.dot(short, jnp.ones((LANES, LANES), jnp.bfloat16), preferred_element_type=jnp.float32)
    base = jnp.dot(above, count.astype(jnp.bfloat16), preferred_element_type=jnp.float32)
    dest = jnp.where(code > 0.0, rank + base, -2.0 * rows)
    grad = grad_ref[...].astype(jnp.float32)
    hess = hess_ref[...].astype(jnp.float32)

    level = lax.broadcasted_iota(jnp.int32, (16, block), 0).astype(jnp.float32)
    slots = [(level + 16.0 * n).astype(jnp.bfloat16) for n in range(block // 16)]
    one = jnp.ones((16, block), jnp.bfloat16)
    zero = jnp.zeros((16, block), jnp.bfloat16)

    def wide_row(array, s):
        return jnp.concatenate([array[i : i + 1, :] for i in range(s * wide, (s + 1) * wide)], axis=1)

    fill = jnp.zeros((13, block), jnp.float32)
    counts = [jnp.sum(member[s * wide : (s + 1) * wide, :]).astype(jnp.int32) for s in range(blocks)]
    done = [jnp.int32(0)]
    for n in counts:
        done.append(done[-1] + n)
    current = jnp.zeros((features + 16, block), jnp.float32)
    bins.wait()
    for s in range(blocks):
        first, last = (lax.div(n, block) for n in done[s : s + 2])
        values = jnp.concatenate(
            [
                arrived[s * block : (s + 1) * block, :].astype(jnp.float32).T,
                wide_row(code, s), wide_row(grad, s), wide_row(hess, s), fill,
            ],
            axis=0,
        ).astype(jnp.bfloat16)
        slot = wide_row(dest, s) - (first * block).astype(jnp.float32)
        moved = []
        for half in range(2):
            near = jnp.broadcast_to(slot - float(half * block), (16, block)).astype(jnp.bfloat16)
            moved += [jnp.where(near == n, one, zero) for n in slots]
        placed = lax.dot_general(
            values, jnp.concatenate(moved, axis=0), (((1,), (1,)), ((), ())),
            preferred_element_type=jnp.float32,
        )
        current = current + placed[:, :block]
        packed[first] = current
        current = jnp.where(last > first, placed[:, block:], current)
    packed[lax.div(done[-1], block)] = current

    for n in range(1, joined):
        packed[lax.div(done[-1], block) + n] = jnp.zeros((features + 16, block), jnp.float32)

    span = joined * block
    sub = lax.broadcasted_iota(jnp.int32, (8, span), 0)
    is_grad = sub < 4
    place = (sub % 4 + 1).astype(jnp.float32)
    level = lax.broadcasted_iota(jnp.int32, (16, span), 0).astype(jnp.float32)
    levels = [(level + 16.0 * n).astype(jnp.bfloat16) for n in range(BINS // 16)]
    one = jnp.ones((16, span), jnp.bfloat16)
    zero = jnp.zeros((16, span), jnp.bfloat16)

    def some_blocks(k, carry):
        def line(i):
            return jnp.concatenate([packed[k * joined + n, i : i + 1, :] for n in range(joined)], axis=1)

        value = jnp.where(is_grad, line(features + 1), line(features + 2))
        owned = line(features) - place
        weights = jnp.concatenate(
            [jnp.where(owned == float(4 * n), value, 0.0) for n in range(leaves // 4)], axis=0
        ).astype(jnp.bfloat16)
        for group in range(features // together):
            upto = []
            for f in range(group * together, (group + 1) * together):
                row = jnp.broadcast_to(line(f), (16, span)).astype(jnp.bfloat16)
                upto += [jnp.where(row <= n, one, zero) for n in levels]
            part = lax.dot_general(
                weights, jnp.concatenate(upto, axis=0), (((1,), (1,)), ((), ())),
                preferred_element_type=jnp.float32,
            )
            for pair in range(together * BINS // LANES):
                owner = group * (together * BINS // LANES) + pair
                for n in range(leaves // 4):
                    out = keep_ref if n < leaves // 8 else send_ref
                    out[n % (leaves // 8), owner] += part[8 * n : 8 * n + 8, pair * LANES : (pair + 1) * LANES]
        return carry

    lax.fori_loop(0, lax.div(done[-1] + (span - 1), span), some_blocks, 0)


def histograms(bin_index, gradient, hessian, child_id, smaller_side, block=256, joined=3, together=4):
    rows, features = bin_index.shape
    leaves = smaller_side.shape[0]
    lines = (rows // LANES, LANES)
    half = pltpu.VMEM((leaves // 8, features * BINS // LANES, 8, LANES), jnp.float32)
    vmem = pl.BlockSpec(memory_space=pltpu.VMEM)
    return pl.pallas_call(
        functools.partial(hist_kernel, block, joined, together),
        out_shape=(half, half),
        in_specs=[pl.BlockSpec(memory_space=pltpu.HBM)] * 5,
        out_specs=(vmem, vmem),
        scratch_shapes=[
            pltpu.SMEM((leaves,), jnp.int32),
            pltpu.VMEM(lines, jnp.bfloat16),
            pltpu.VMEM(lines, jnp.bfloat16),
            pltpu.VMEM(lines, jnp.int32),
            pltpu.VMEM((rows, features), jnp.int32),
            pltpu.VMEM((rows // block + joined, features + 16, block), jnp.float32),
            pltpu.SemaphoreType.DMA((5,)),
        ],
        compiler_params=pltpu.CompilerParams(vmem_limit_bytes=40 * 2**20),
        name="histograms",
    )(
        *(
            pltpu.with_memory_space_constraint(a, pltpu.HBM)
            for a in (
                smaller_side, bin_index,
                gradient.reshape(lines), hessian.reshape(lines), child_id.reshape(lines),
            )
        )
    )


def gain_kernel(pieces_ref, best_ref, told_ref):
    left = jnp.sum(pieces_ref[...], axis=0)
    lane = lax.broadcasted_iota(jnp.int32, (8, LANES), 1)
    first = jnp.sum(jnp.where(lane == BINS - 1, left, 0.0), axis=1, keepdims=True)
    second = jnp.sum(jnp.where(lane == 2 * BINS - 1, left, 0.0), axis=1, keepdims=True)
    total = jnp.where(lane < BINS, first, second)
    left_grad, left_hess = left[:4], left[4:]
    total_grad, total_hess = total[:4], total[4:]
    right_grad = total_grad - left_grad
    value = left_grad * left_grad / (left_hess + reg_lambda)
    value = value + right_grad * right_grad / (total_hess - left_hess + reg_lambda)
    value = value - total_grad * total_grad / (total_hess + reg_lambda)
    lane = lane[:4]
    bottom = jnp.float32(-jnp.inf)
    inner = lane % BINS < BINS - 1
    one = jnp.max(jnp.where(inner & (lane < BINS), value, bottom), axis=1, keepdims=True)
    two = jnp.max(jnp.where(inner & (lane >= BINS), value, bottom), axis=1, keepdims=True)
    best_ref[...] = jnp.concatenate([one, two], axis=1)
    diagonal = lane == lax.broadcasted_iota(jnp.int32, (4, LANES), 0)
    told = jnp.sum(jnp.where(diagonal, jnp.maximum(one, two), 0.0), axis=0, keepdims=True)
    told_ref[...] = jnp.broadcast_to(told, told_ref.shape)


def gains(pieces, listeners):
    vmem = pl.BlockSpec(memory_space=pltpu.VMEM)
    return pl.pallas_call(
        gain_kernel,
        out_shape=(
            jax.ShapeDtypeStruct((4, 2), jnp.float32),
            jax.ShapeDtypeStruct((listeners, LANES), jnp.float32),
        ),
        in_specs=[vmem],
        out_specs=(vmem, vmem),
        compiler_params=pltpu.CompilerParams(vmem_limit_bytes=4 * 2**20),
        name="gains",
    )(pieces)


def body(bin_index, gradient, hessian, child_id, smaller_side):
    ny, nc, nx, nz = (lax.axis_size(a) for a in AXES)
    keep, send = histograms(bin_index, gradient, hessian, child_id, smaller_side)
    chip = keep + lax.ppermute(send, "core", [(0, 1), (1, 0)])
    chip = chip.reshape(ny * nx, nz, 8, LANES)
    plane = jnp.sum(lax.all_to_all(chip, ("y", "x"), 0, 0, tiled=True), axis=0)
    pieces = lax.all_to_all(plane, "z", 0, 0, tiled=True)
    best_gain, told = gains(pieces, nx * nz)
    heard = lax.all_to_all(told, ("x", "z"), 0, 0, tiled=True)
    child_best = jnp.max(heard, axis=0)[:4]
    return best_gain, child_best


def solution(mesh):
    split = Mesh(mesh.devices.reshape(4, 2, 4, 16), AXES)
    every = P(AXES)
    return jax.shard_map(
        body,
        mesh=split,
        in_specs=(P(AXES, None), every, every, every, P()),
        out_specs=(P(("y", "core"), ("x", "z")), P(("y", "core"))),
        check_vma=False,
    )
```

```python
import functools

import jax
import jax.numpy as jnp
from jax import lax
from jax.experimental import pallas as pl
from jax.experimental.pallas import tpu as pltpu
from jax.sharding import Mesh
from jax.sharding import PartitionSpec as P

BINS = 64
LANES = 128
AXES = ("y", "core", "x", "zh", "zm", "zp")
Z_PARTS = (4, 2, 2)
reg_lambda = 1.0


def position(owner):
    x, zh, zm, zp = owner // 16, owner // 4 % 4, owner // 2 % 2, owner % 2
    return x * 16 + zp * 8 + zm * 4 + zh


def hist_kernel(block, joined, together, side_hbm, bin_ref, grad_hbm, hess_hbm, child_hbm,
                keep_ref, send_ref, side_ref, grad_ref, hess_ref, child_ref, arrived, packed, copied):
    rows, features = bin_ref.shape
    leaves = side_ref.shape[0]
    blocks = rows // block
    wide = block // LANES
    bins = pltpu.make_async_copy(bin_ref, arrived, copied.at[4])
    small = [
        pltpu.make_async_copy(source, target, copied.at[i])
        for i, (source, target) in enumerate(
            [(side_hbm, side_ref), (child_hbm, child_ref), (grad_hbm, grad_ref), (hess_hbm, hess_ref)]
        )
    ]
    for copy in small + [bins]:
        copy.start()
    keep_ref[...] = jnp.zeros_like(keep_ref)
    send_ref[...] = jnp.zeros_like(send_ref)

    for copy in small:
        copy.wait()
    mine = lax.axis_index("core")
    child = child_ref[...]
    code = jnp.zeros(child.shape, jnp.int32)
    for leaf in range(leaves):
        y, core, low = leaf // 8, leaf // 4 % 2, leaf % 4
        place = (core ^ mine) * (leaves // 2) + y * 4 + low
        code = jnp.where(child == 2 * leaf + side_ref[leaf], place + 1, code)
    code = code.astype(jnp.float32)
    member = jnp.where(code > 0.0, 1.0, 0.0)

    lane = [lax.broadcasted_iota(jnp.int32, (LANES, LANES), d) for d in (0, 1)]
    before = jnp.where(lane[0] < lane[1], 1.0, 0.0).astype(jnp.bfloat16)
    lines = child.shape[0]
    line = [lax.broadcasted_iota(jnp.int32, (lines, lines), d) for d in (0, 1)]
    above = jnp.where(line[1] < line[0], 1.0, 0.0).astype(jnp.bfloat16)
    short = member.astype(jnp.bfloat16)
    rank = jnp.dot(short, before, preferred_element_type=jnp.float32)
    count = jnp.dot(short, jnp.ones((LANES, LANES), jnp.bfloat16), preferred_element_type=jnp.float32)
    base = jnp.dot(above, count.astype(jnp.bfloat16), preferred_element_type=jnp.float32)
    dest = jnp.where(code > 0.0, rank + base, -2.0 * rows)
    grad = grad_ref[...].astype(jnp.float32)
    hess = hess_ref[...].astype(jnp.float32)

    level = lax.broadcasted_iota(jnp.int32, (16, block), 0).astype(jnp.float32)
    slots = [(level + 16.0 * n).astype(jnp.bfloat16) for n in range(block // 16)]
    one = jnp.ones((16, block), jnp.bfloat16)
    zero = jnp.zeros((16, block), jnp.bfloat16)

    def wide_row(array, s):
        return jnp.concatenate([array[i : i + 1, :] for i in range(s * wide, (s + 1) * wide)], axis=1)

    fill = jnp.zeros((13, block), jnp.float32)
    counts = [jnp.sum(member[s * wide : (s + 1) * wide, :]).astype(jnp.int32) for s in range(blocks)]
    done = [jnp.int32(0)]
    for n in counts:
        done.append(done[-1] + n)
    current = jnp.zeros((features + 16, block), jnp.float32)
    bins.wait()
    for s in range(blocks):
        first, last = (lax.div(n, block) for n in done[s : s + 2])
        values = jnp.concatenate(
            [
                arrived[s * block : (s + 1) * block, :].astype(jnp.float32).T,
                wide_row(code, s), wide_row(grad, s), wide_row(hess, s), fill,
            ],
            axis=0,
        ).astype(jnp.bfloat16)
        slot = wide_row(dest, s) - (first * block).astype(jnp.float32)
        moved = []
        for half in range(2):
            near = jnp.broadcast_to(slot - float(half * block), (16, block)).astype(jnp.bfloat16)
            moved += [jnp.where(near == n, one, zero) for n in slots]
        placed = lax.dot_general(
            values, jnp.concatenate(moved, axis=0), (((1,), (1,)), ((), ())),
            preferred_element_type=jnp.float32,
        )
        current = current + placed[:, :block]
        packed[first] = current
        current = jnp.where(last > first, placed[:, block:], current)
    packed[lax.div(done[-1], block)] = current

    for n in range(1, joined):
        packed[lax.div(done[-1], block) + n] = jnp.zeros((features + 16, block), jnp.float32)

    span = joined * block
    sub = lax.broadcasted_iota(jnp.int32, (8, span), 0)
    is_grad = sub < 4
    place = (sub % 4 + 1).astype(jnp.float32)
    level = lax.broadcasted_iota(jnp.int32, (16, span), 0).astype(jnp.float32)
    levels = [(level + 16.0 * n).astype(jnp.bfloat16) for n in range(BINS // 16)]
    one = jnp.ones((16, span), jnp.bfloat16)
    zero = jnp.zeros((16, span), jnp.bfloat16)

    def some_blocks(k, carry):
        def line(i):
            return jnp.concatenate([packed[k * joined + n, i : i + 1, :] for n in range(joined)], axis=1)

        value = jnp.where(is_grad, line(features + 1), line(features + 2))
        owned = line(features) - place
        weights = jnp.concatenate(
            [jnp.where(owned == float(4 * n), value, 0.0) for n in range(leaves // 4)], axis=0
        ).astype(jnp.bfloat16)
        for group in range(features // together):
            upto = []
            for f in range(group * together, (group + 1) * together):
                row = jnp.broadcast_to(line(f), (16, span)).astype(jnp.bfloat16)
                upto += [jnp.where(row <= n, one, zero) for n in levels]
            part = lax.dot_general(
                weights, jnp.concatenate(upto, axis=0), (((1,), (1,)), ((), ())),
                preferred_element_type=jnp.float32,
            )
            for pair in range(together * BINS // LANES):
                owner = group * (together * BINS // LANES) + pair
                for n in range(leaves // 4):
                    out = keep_ref if n < leaves // 8 else send_ref
                    out[n % (leaves // 8), position(owner)] += part[8 * n : 8 * n + 8, pair * LANES : (pair + 1) * LANES]
        return carry

    lax.fori_loop(0, lax.div(done[-1] + (span - 1), span), some_blocks, 0)


def histograms(bin_index, gradient, hessian, child_id, smaller_side, block=256, joined=3, together=4):
    rows, features = bin_index.shape
    leaves = smaller_side.shape[0]
    lines = (rows // LANES, LANES)
    half = pltpu.VMEM((leaves // 8, features * BINS // LANES, 8, LANES), jnp.float32)
    vmem = pl.BlockSpec(memory_space=pltpu.VMEM)
    return pl.pallas_call(
        functools.partial(hist_kernel, block, joined, together),
        out_shape=(half, half),
        in_specs=[pl.BlockSpec(memory_space=pltpu.HBM)] * 5,
        out_specs=(vmem, vmem),
        scratch_shapes=[
            pltpu.SMEM((leaves,), jnp.int32),
            pltpu.VMEM(lines, jnp.bfloat16),
            pltpu.VMEM(lines, jnp.bfloat16),
            pltpu.VMEM(lines, jnp.int32),
            pltpu.VMEM((rows, features), jnp.int32),
            pltpu.VMEM((rows // block + joined, features + 16, block), jnp.float32),
            pltpu.SemaphoreType.DMA((5,)),
        ],
        compiler_params=pltpu.CompilerParams(vmem_limit_bytes=40 * 2**20),
        name="histograms",
    )(
        *(
            pltpu.with_memory_space_constraint(a, pltpu.HBM)
            for a in (
                smaller_side, bin_index,
                gradient.reshape(lines), hessian.reshape(lines), child_id.reshape(lines),
            )
        )
    )


def gain_kernel(pieces_ref, best_ref, told_ref):
    tiles = pieces_ref.shape[1]
    mine = lax.axis_index("zh")
    left = jnp.sum(pieces_ref[...], axis=0)
    best = [tile_gains(left[t]) for t in range(tiles)]
    one, two = best[0]
    highest = jnp.maximum(one, two)
    for t in range(1, tiles):
        one = jnp.where(mine == t, best[t][0], one)
        two = jnp.where(mine == t, best[t][1], two)
        highest = jnp.maximum(highest, jnp.maximum(*best[t]))
    best_ref[...] = jnp.concatenate([one, two], axis=1)
    lane, leaf = (lax.broadcasted_iota(jnp.int32, (4, LANES), d) for d in (1, 0))
    told = jnp.sum(jnp.where(lane == leaf, highest, 0.0), axis=0, keepdims=True)
    told_ref[...] = jnp.broadcast_to(told, told_ref.shape)


def tile_gains(left):
    lane = lax.broadcasted_iota(jnp.int32, (8, LANES), 1)
    first = jnp.sum(jnp.where(lane == BINS - 1, left, 0.0), axis=1, keepdims=True)
    second = jnp.sum(jnp.where(lane == 2 * BINS - 1, left, 0.0), axis=1, keepdims=True)
    total = jnp.where(lane < BINS, first, second)
    left_grad, left_hess = left[:4], left[4:]
    total_grad, total_hess = total[:4], total[4:]
    right_grad = total_grad - left_grad
    value = left_grad * left_grad / (left_hess + reg_lambda)
    value = value + right_grad * right_grad / (total_hess - left_hess + reg_lambda)
    value = value - total_grad * total_grad / (total_hess + reg_lambda)
    lane = lane[:4]
    bottom = jnp.float32(-jnp.inf)
    inner = lane % BINS < BINS - 1
    one = jnp.max(jnp.where(inner & (lane < BINS), value, bottom), axis=1, keepdims=True)
    two = jnp.max(jnp.where(inner & (lane >= BINS), value, bottom), axis=1, keepdims=True)
    return one, two


def gains(pieces, listeners):
    vmem = pl.BlockSpec(memory_space=pltpu.VMEM)
    return pl.pallas_call(
        gain_kernel,
        out_shape=(
            jax.ShapeDtypeStruct((4, 2), jnp.float32),
            jax.ShapeDtypeStruct((listeners, LANES), jnp.float32),
        ),
        in_specs=[vmem],
        out_specs=(vmem, vmem),
        compiler_params=pltpu.CompilerParams(vmem_limit_bytes=4 * 2**20),
        name="gains",
    )(pieces)


def body(bin_index, gradient, hessian, child_id, smaller_side):
    ny, nc, nx, nh, nm, np_ = (lax.axis_size(a) for a in AXES)
    keep, send = histograms(bin_index, gradient, hessian, child_id, smaller_side)
    chip = keep + lax.ppermute(send, "core", [(0, 1), (1, 0)])
    chip = chip.reshape(ny * nx * np_, nm * nh, 8, LANES)
    near = jnp.sum(lax.all_to_all(chip, ("y", "x", "zp"), 0, 0, tiled=True), axis=0)
    near = jnp.broadcast_to(near.reshape(nm, 1, nh, 8, LANES), (nm, nh, nh, 8, LANES))
    pieces = lax.all_to_all(near.reshape(nm * nh, nh, 8, LANES), ("zm", "zh"), 0, 0, tiled=True)
    best_gain, told = gains(pieces, nx * nm * np_)
    heard = lax.all_to_all(told, ("x", "zm", "zp"), 0, 0, tiled=True)
    child_best = jnp.max(heard, axis=0)[:4]
    return best_gain, child_best


def solution(mesh):
    split = Mesh(mesh.devices.reshape(4, 2, 4, *Z_PARTS), AXES)
    every = P(AXES)
    return jax.shard_map(
        body,
        mesh=split,
        in_specs=(P(AXES, None), every, every, every, P()),
        out_specs=(P(("y", "core"), ("x", "zh", "zm", "zp")), P(("y", "core"))),
        check_vma=False,
    )
```

```python
import functools

import jax
import jax.numpy as jnp
from jax import lax
from jax.experimental import pallas as pl
from jax.experimental.pallas import tpu as pltpu
from jax.sharding import Mesh
from jax.sharding import PartitionSpec as P

BINS = 64
LANES = 128
AXES = ("y", "core", "x", "zh", "zm", "zp")
Z_PARTS = (4, 2, 2)
reg_lambda = 1.0


def position(owner):
    x, zh, zm, zp = owner // 16, owner // 4 % 4, owner // 2 % 2, owner % 2
    return x * 16 + zp * 8 + zm * 4 + zh


def hist_kernel(block, joined, together, side_hbm, bin_ref, grad_hbm, hess_hbm, child_hbm,
                keep_ref, send_ref, side_ref, grad_ref, hess_ref, child_ref, arrived, packed, odd_sums, copied):
    rows, features = bin_ref.shape
    leaves = side_ref.shape[0]
    blocks = rows // block
    wide = block // LANES
    bins = pltpu.make_async_copy(bin_ref, arrived, copied.at[4])
    small = [
        pltpu.make_async_copy(source, target, copied.at[i])
        for i, (source, target) in enumerate(
            [(side_hbm, side_ref), (child_hbm, child_ref), (grad_hbm, grad_ref), (hess_hbm, hess_ref)]
        )
    ]
    for copy in small + [bins]:
        copy.start()
    for ref in (keep_ref, send_ref, odd_sums):
        ref[...] = jnp.zeros_like(ref)

    for copy in small:
        copy.wait()
    mine = lax.axis_index("core")
    child = child_ref[...]
    code = jnp.zeros(child.shape, jnp.int32)
    for leaf in range(leaves):
        y, core, low = leaf // 8, leaf // 4 % 2, leaf % 4
        place = (core ^ mine) * (leaves // 2) + y * 4 + low
        code = jnp.where(child == 2 * leaf + side_ref[leaf], place + 1, code)
    code = code.astype(jnp.float32)
    member = jnp.where(code > 0.0, 1.0, 0.0)

    lane = [lax.broadcasted_iota(jnp.int32, (LANES, LANES), d) for d in (0, 1)]
    before = jnp.where(lane[0] < lane[1], 1.0, 0.0).astype(jnp.bfloat16)
    lines = child.shape[0]
    line = [lax.broadcasted_iota(jnp.int32, (lines, lines), d) for d in (0, 1)]
    above = jnp.where(line[1] < line[0], 1.0, 0.0).astype(jnp.bfloat16)
    short = member.astype(jnp.bfloat16)
    rank = jnp.dot(short, before, preferred_element_type=jnp.float32)
    count = jnp.dot(short, jnp.ones((LANES, LANES), jnp.bfloat16), preferred_element_type=jnp.float32)
    base = jnp.dot(above, count.astype(jnp.bfloat16), preferred_element_type=jnp.float32)
    dest = jnp.where(code > 0.0, rank + base, -2.0 * rows)
    grad = grad_ref[...].astype(jnp.float32)
    hess = hess_ref[...].astype(jnp.float32)

    level = lax.broadcasted_iota(jnp.int32, (16, block), 0).astype(jnp.float32)
    slots = [(level + 16.0 * n).astype(jnp.bfloat16) for n in range(block // 16)]
    one = jnp.ones((16, block), jnp.bfloat16)
    zero = jnp.zeros((16, block), jnp.bfloat16)

    def wide_row(array, s):
        return jnp.concatenate([array[i : i + 1, :] for i in range(s * wide, (s + 1) * wide)], axis=1)

    fill = jnp.zeros((13, block), jnp.float32)
    counts = [jnp.sum(member[s * wide : (s + 1) * wide, :]).astype(jnp.int32) for s in range(blocks)]
    done = [jnp.int32(0)]
    for n in counts:
        done.append(done[-1] + n)
    current = jnp.zeros((features + 16, block), jnp.float32)
    bins.wait()
    for s in range(blocks):
        first, last = (lax.div(n, block) for n in done[s : s + 2])
        values = jnp.concatenate(
            [
                arrived[s * block : (s + 1) * block, :].astype(jnp.float32).T,
                wide_row(code, s), wide_row(grad, s), wide_row(hess, s), fill,
            ],
            axis=0,
        ).astype(jnp.bfloat16)
        slot = wide_row(dest, s) - (first * block).astype(jnp.float32)
        moved = []
        for half in range(2):
            near = jnp.broadcast_to(slot - float(half * block), (16, block)).astype(jnp.bfloat16)
            moved += [jnp.where(near == n, one, zero) for n in slots]
        placed = lax.dot_general(
            values, jnp.concatenate(moved, axis=0), (((1,), (1,)), ((), ())),
            preferred_element_type=jnp.float32,
        )
        current = current + placed[:, :block]
        packed[first] = current
        current = jnp.where(last > first, placed[:, block:], current)
    packed[lax.div(done[-1], block)] = current

    for n in range(1, joined):
        packed[lax.div(done[-1], block) + n] = jnp.zeros((features + 16, block), jnp.float32)

    sub = lax.broadcasted_iota(jnp.int32, (8, block), 0)
    is_grad = sub < 4
    place = (sub % 4 + 1).astype(jnp.float32)
    levels = slots[: BINS // 16]
    groups = features // together
    tiles = together * BINS // LANES
    contract = (((1,), (1,)), ((), ()))

    def out_tile(owner, n):
        return (keep_ref if n < leaves // 8 else send_ref).at[n % (leaves // 8), position(owner)]

    def some_blocks(step, carry):
        for k in (step * joined + n for n in range(joined)):
            value = jnp.where(
                is_grad,
                packed[k, features + 1 : features + 2, :],
                packed[k, features + 2 : features + 3, :],
            )
            owned = packed[k, features : features + 1, :] - place
            weights = jnp.concatenate(
                [jnp.where(owned == float(4 * n), value, 0.0) for n in range(leaves // 4)], axis=0
            ).astype(jnp.bfloat16)
            for group in range(groups):
                upto = []
                for f in range(group * together, (group + 1) * together):
                    row = jnp.broadcast_to(packed[k, f : f + 1, :], (16, block)).astype(jnp.bfloat16)
                    upto += [jnp.where(row <= n, one, zero) for n in levels]
                upto = jnp.concatenate(upto, axis=0)
                if group % 2:
                    odd_sums[group // 2] += lax.dot_general(
                        upto, weights, contract, preferred_element_type=jnp.float32
                    )
                    continue
                part = lax.dot_general(weights, upto, contract, preferred_element_type=jnp.float32)
                for tile in range(tiles):
                    for n in range(leaves // 4):
                        out = out_tile(group * tiles + tile, n)
                        out[...] += part[8 * n : 8 * n + 8, tile * LANES : (tile + 1) * LANES]
        return carry

    span = joined * block
    lax.fori_loop(0, lax.div(done[-1] + (span - 1), span), some_blocks, 0)
    for group in range(1, groups, 2):
        for tile in range(tiles):
            part = odd_sums[group // 2, tile * LANES : (tile + 1) * LANES, :].T
            for n in range(leaves // 4):
                out = out_tile(group * tiles + tile, n)
                out[...] = part[8 * n : 8 * n + 8, :]


def histograms(bin_index, gradient, hessian, child_id, smaller_side, block=256, joined=3, together=4):
    rows, features = bin_index.shape
    leaves = smaller_side.shape[0]
    lines = (rows // LANES, LANES)
    half = pltpu.VMEM((leaves // 8, features * BINS // LANES, 8, LANES), jnp.float32)
    vmem = pl.BlockSpec(memory_space=pltpu.VMEM)
    return pl.pallas_call(
        functools.partial(hist_kernel, block, joined, together),
        out_shape=(half, half),
        in_specs=[pl.BlockSpec(memory_space=pltpu.HBM)] * 5,
        out_specs=(vmem, vmem),
        scratch_shapes=[
            pltpu.SMEM((leaves,), jnp.int32),
            pltpu.VMEM(lines, jnp.bfloat16),
            pltpu.VMEM(lines, jnp.bfloat16),
            pltpu.VMEM(lines, jnp.int32),
            pltpu.VMEM((rows, features), jnp.int32),
            pltpu.VMEM((rows // block + joined, features + 16, block), jnp.float32),
            pltpu.VMEM((features // together // 2, together * BINS, 2 * leaves), jnp.float32),
            pltpu.SemaphoreType.DMA((5,)),
        ],
        compiler_params=pltpu.CompilerParams(vmem_limit_bytes=40 * 2**20),
        name="histograms",
    )(
        *(
            pltpu.with_memory_space_constraint(a, pltpu.HBM)
            for a in (
                smaller_side, bin_index,
                gradient.reshape(lines), hessian.reshape(lines), child_id.reshape(lines),
            )
        )
    )


def gain_kernel(pieces_ref, best_ref, told_ref):
    tiles = pieces_ref.shape[1]
    mine = lax.axis_index("zh")
    left = jnp.sum(pieces_ref[...], axis=0)
    best = [tile_gains(left[t]) for t in range(tiles)]
    one, two = best[0]
    highest = jnp.maximum(one, two)
    for t in range(1, tiles):
        one = jnp.where(mine == t, best[t][0], one)
        two = jnp.where(mine == t, best[t][1], two)
        highest = jnp.maximum(highest, jnp.maximum(*best[t]))
    best_ref[...] = jnp.concatenate([one, two], axis=1)
    lane, leaf = (lax.broadcasted_iota(jnp.int32, (4, LANES), d) for d in (1, 0))
    told = jnp.sum(jnp.where(lane == leaf, highest, 0.0), axis=0, keepdims=True)
    told_ref[...] = jnp.broadcast_to(told, told_ref.shape)


def tile_gains(left):
    lane = lax.broadcasted_iota(jnp.int32, (8, LANES), 1)
    first = jnp.sum(jnp.where(lane == BINS - 1, left, 0.0), axis=1, keepdims=True)
    second = jnp.sum(jnp.where(lane == 2 * BINS - 1, left, 0.0), axis=1, keepdims=True)
    total = jnp.where(lane < BINS, first, second)
    left_grad, left_hess = left[:4], left[4:]
    total_grad, total_hess = total[:4], total[4:]
    right_grad = total_grad - left_grad
    value = left_grad * left_grad / (left_hess + reg_lambda)
    value = value + right_grad * right_grad / (total_hess - left_hess + reg_lambda)
    value = value - total_grad * total_grad / (total_hess + reg_lambda)
    lane = lane[:4]
    bottom = jnp.float32(-jnp.inf)
    inner = lane % BINS < BINS - 1
    one = jnp.max(jnp.where(inner & (lane < BINS), value, bottom), axis=1, keepdims=True)
    two = jnp.max(jnp.where(inner & (lane >= BINS), value, bottom), axis=1, keepdims=True)
    return one, two


def gains(pieces, listeners):
    vmem = pl.BlockSpec(memory_space=pltpu.VMEM)
    return pl.pallas_call(
        gain_kernel,
        out_shape=(
            jax.ShapeDtypeStruct((4, 2), jnp.float32),
            jax.ShapeDtypeStruct((listeners, LANES), jnp.float32),
        ),
        in_specs=[vmem],
        out_specs=(vmem, vmem),
        compiler_params=pltpu.CompilerParams(vmem_limit_bytes=4 * 2**20),
        name="gains",
    )(pieces)


def body(bin_index, gradient, hessian, child_id, smaller_side):
    ny, nc, nx, nh, nm, np_ = (lax.axis_size(a) for a in AXES)
    keep, send = histograms(bin_index, gradient, hessian, child_id, smaller_side)
    chip = keep + lax.ppermute(send, "core", [(0, 1), (1, 0)])
    chip = chip.reshape(ny * nx * np_, nm * nh, 8, LANES)
    near = jnp.sum(lax.all_to_all(chip, ("y", "x", "zp"), 0, 0, tiled=True), axis=0)
    near = jnp.broadcast_to(near.reshape(nm, 1, nh, 8, LANES), (nm, nh, nh, 8, LANES))
    pieces = lax.all_to_all(near.reshape(nm * nh, nh, 8, LANES), ("zm", "zh"), 0, 0, tiled=True)
    best_gain, told = gains(pieces, nx * nm * np_)
    heard = lax.all_to_all(told, ("x", "zm", "zp"), 0, 0, tiled=True)
    child_best = jnp.max(heard, axis=0)[:4]
    return best_gain, child_best


def solution(mesh):
    split = Mesh(mesh.devices.reshape(4, 2, 4, *Z_PARTS), AXES)
    every = P(AXES)
    return jax.shard_map(
        body,
        mesh=split,
        in_specs=(P(AXES, None), every, every, every, P()),
        out_specs=(P(("y", "core"), ("x", "zh", "zm", "zp")), P(("y", "core"))),
        check_vma=False,
    )
```

```python
import functools

import jax
import jax.numpy as jnp
from jax import lax
from jax.experimental import pallas as pl
from jax.experimental.pallas import tpu as pltpu
from jax.sharding import Mesh
from jax.sharding import PartitionSpec as P

BINS = 64
LANES = 128
AXES = ("y", "core", "x", "zh", "zm", "zp")
Z_PARTS = (4, 2, 2)
reg_lambda = 1.0


def position(owner):
    x, zh, zm, zp = owner // 16, owner // 4 % 4, owner // 2 % 2, owner % 2
    return x * 16 + zp * 8 + zm * 4 + zh


def hist_kernel(block, joined, together, side_hbm, bin_ref, grad_hbm, hess_hbm, child_hbm,
                keep_ref, send_ref, side_ref, grad_ref, hess_ref, child_ref, arrived, packed, odd_sums, copied):
    rows, features = bin_ref.shape
    leaves = side_ref.shape[0]
    blocks = rows // block
    wide = block // LANES
    bins = pltpu.make_async_copy(bin_ref, arrived, copied.at[4])
    small = [
        pltpu.make_async_copy(source, target, copied.at[i])
        for i, (source, target) in enumerate(
            [(side_hbm, side_ref), (child_hbm, child_ref), (grad_hbm, grad_ref), (hess_hbm, hess_ref)]
        )
    ]
    for copy in small + [bins]:
        copy.start()
    odd_sums[...] = jnp.zeros_like(odd_sums)
    tiles = together * BINS // LANES
    for owner in range(features * BINS // LANES):
        if owner // tiles % 2 == 0:
            for ref in (keep_ref, send_ref):
                ref[:, position(owner)] = jnp.zeros((leaves // 8, 8, LANES), jnp.float32)

    for copy in small:
        copy.wait()
    mine = lax.axis_index("core")
    child = child_ref[...]
    code = jnp.zeros(child.shape, jnp.int32)
    for leaf in range(leaves):
        y, core, low = leaf // 8, leaf // 4 % 2, leaf % 4
        place = (core ^ mine) * (leaves // 2) + y * 4 + low
        code = jnp.where(child == 2 * leaf + side_ref[leaf], place + 1, code)
    code = code.astype(jnp.float32)
    member = jnp.where(code > 0.0, 1.0, 0.0)

    lane = [lax.broadcasted_iota(jnp.int32, (LANES, LANES), d) for d in (0, 1)]
    before = jnp.where(lane[0] < lane[1], 1.0, 0.0).astype(jnp.bfloat16)
    lines = child.shape[0]
    line = [lax.broadcasted_iota(jnp.int32, (lines, lines), d) for d in (0, 1)]
    above = jnp.where(line[1] < line[0], 1.0, 0.0).astype(jnp.bfloat16)
    short = member.astype(jnp.bfloat16)
    rank = jnp.dot(short, before, preferred_element_type=jnp.float32)
    count = jnp.dot(short, jnp.ones((LANES, LANES), jnp.bfloat16), preferred_element_type=jnp.float32)
    base = jnp.dot(above, count.astype(jnp.bfloat16), preferred_element_type=jnp.float32)
    dest = jnp.where(code > 0.0, rank + base, -2.0 * rows)
    grad = grad_ref[...].astype(jnp.float32)
    hess = hess_ref[...].astype(jnp.float32)

    level = lax.broadcasted_iota(jnp.int32, (16, block), 0).astype(jnp.float32)
    slots = [(level + 16.0 * n).astype(jnp.bfloat16) for n in range(block // 16)]
    one = jnp.ones((16, block), jnp.bfloat16)
    zero = jnp.zeros((16, block), jnp.bfloat16)

    def wide_row(array, s):
        return jnp.concatenate([array[i : i + 1, :] for i in range(s * wide, (s + 1) * wide)], axis=1)

    fill = jnp.zeros((13, block), jnp.float32)
    counts = [jnp.sum(member[s * wide : (s + 1) * wide, :]).astype(jnp.int32) for s in range(blocks)]
    done = [jnp.int32(0)]
    for n in counts:
        done.append(done[-1] + n)
    current = jnp.zeros((features + 16, block), jnp.float32)
    bins.wait()
    for s in range(blocks):
        first, last = (lax.div(n, block) for n in done[s : s + 2])
        values = jnp.concatenate(
            [
                arrived[s * block : (s + 1) * block, :].astype(jnp.float32).T,
                wide_row(code, s), wide_row(grad, s), wide_row(hess, s), fill,
            ],
            axis=0,
        ).astype(jnp.bfloat16)
        slot = wide_row(dest, s) - (first * block).astype(jnp.float32)
        moved = []
        for half in range(2):
            near = jnp.broadcast_to(slot - float(half * block), (16, block)).astype(jnp.bfloat16)
            moved += [jnp.where(near == n, one, zero) for n in slots]
        placed = lax.dot_general(
            values, jnp.concatenate(moved, axis=0), (((1,), (1,)), ((), ())),
            preferred_element_type=jnp.float32,
        )
        current = current + placed[:, :block]
        packed[first] = current
        current = jnp.where(last > first, placed[:, block:], current)
    packed[lax.div(done[-1], block)] = current

    for n in range(1, joined):
        packed[lax.div(done[-1], block) + n] = jnp.zeros((features + 16, block), jnp.float32)

    sub = lax.broadcasted_iota(jnp.int32, (8, block), 0)
    is_grad = sub < 4
    place = (sub % 4 + 1).astype(jnp.float32)
    levels = slots[: BINS // 16]
    groups = features // together
    contract = (((1,), (1,)), ((), ()))

    def out_tile(owner, n):
        return (keep_ref if n < leaves // 8 else send_ref).at[n % (leaves // 8), position(owner)]

    def some_blocks(step, carry):
        for k in (step * joined + n for n in range(joined)):
            value = jnp.where(
                is_grad,
                packed[k, features + 1 : features + 2, :],
                packed[k, features + 2 : features + 3, :],
            )
            owned = packed[k, features : features + 1, :] - place
            weights = jnp.concatenate(
                [jnp.where(owned == float(4 * n), value, 0.0) for n in range(leaves // 4)], axis=0
            ).astype(jnp.bfloat16)
            for group in range(groups):
                upto = []
                for f in range(group * together, (group + 1) * together):
                    row = jnp.broadcast_to(packed[k, f : f + 1, :], (16, block)).astype(jnp.bfloat16)
                    upto += [jnp.where(row <= n, one, zero) for n in levels]
                upto = jnp.concatenate(upto, axis=0)
                if group % 2:
                    odd_sums[group // 2] += lax.dot_general(
                        upto, weights, contract, preferred_element_type=jnp.float32
                    )
                    continue
                part = lax.dot_general(weights, upto, contract, preferred_element_type=jnp.float32)
                for tile in range(tiles):
                    for n in range(leaves // 4):
                        out = out_tile(group * tiles + tile, n)
                        out[...] += part[8 * n : 8 * n + 8, tile * LANES : (tile + 1) * LANES]
        return carry

    span = joined * block
    lax.fori_loop(0, lax.div(done[-1] + (span - 1), span), some_blocks, 0)
    for group in range(1, groups, 2):
        for tile in range(tiles):
            part = odd_sums[group // 2, tile * LANES : (tile + 1) * LANES, :].T
            for n in range(leaves // 4):
                out = out_tile(group * tiles + tile, n)
                out[...] = part[8 * n : 8 * n + 8, :]


def histograms(bin_index, gradient, hessian, child_id, smaller_side, block=256, joined=3, together=4):
    rows, features = bin_index.shape
    leaves = smaller_side.shape[0]
    lines = (rows // LANES, LANES)
    half = pltpu.VMEM((leaves // 8, features * BINS // LANES, 8, LANES), jnp.float32)
    vmem = pl.BlockSpec(memory_space=pltpu.VMEM)
    return pl.pallas_call(
        functools.partial(hist_kernel, block, joined, together),
        out_shape=(half, half),
        in_specs=[pl.BlockSpec(memory_space=pltpu.HBM)] * 5,
        out_specs=(vmem, vmem),
        scratch_shapes=[
            pltpu.SMEM((leaves,), jnp.int32),
            pltpu.VMEM(lines, jnp.bfloat16),
            pltpu.VMEM(lines, jnp.bfloat16),
            pltpu.VMEM(lines, jnp.int32),
            pltpu.VMEM((rows, features), jnp.int32),
            pltpu.VMEM((rows // block + joined, features + 16, block), jnp.float32),
            pltpu.VMEM((features // together // 2, together * BINS, 2 * leaves), jnp.float32),
            pltpu.SemaphoreType.DMA((5,)),
        ],
        compiler_params=pltpu.CompilerParams(vmem_limit_bytes=40 * 2**20),
        name="histograms",
    )(
        *(
            pltpu.with_memory_space_constraint(a, pltpu.HBM)
            for a in (
                smaller_side, bin_index,
                gradient.reshape(lines), hessian.reshape(lines), child_id.reshape(lines),
            )
        )
    )


def gain_kernel(pieces_ref, best_ref, told_ref):
    tiles = pieces_ref.shape[1]
    mine = lax.axis_index("zh")
    left = jnp.sum(pieces_ref[...], axis=0)
    best = [tile_gains(left[t]) for t in range(tiles)]
    one, two = best[0]
    highest = jnp.maximum(one, two)
    for t in range(1, tiles):
        one = jnp.where(mine == t, best[t][0], one)
        two = jnp.where(mine == t, best[t][1], two)
        highest = jnp.maximum(highest, jnp.maximum(*best[t]))
    best_ref[...] = jnp.concatenate([one, two], axis=1)
    lane, leaf = (lax.broadcasted_iota(jnp.int32, (4, LANES), d) for d in (1, 0))
    told = jnp.sum(jnp.where(lane == leaf, highest, 0.0), axis=0, keepdims=True)
    told_ref[...] = jnp.broadcast_to(told, told_ref.shape)


def tile_gains(left):
    lane = lax.broadcasted_iota(jnp.int32, (8, LANES), 1)
    first = jnp.sum(jnp.where(lane == BINS - 1, left, 0.0), axis=1, keepdims=True)
    second = jnp.sum(jnp.where(lane == 2 * BINS - 1, left, 0.0), axis=1, keepdims=True)
    total = jnp.where(lane < BINS, first, second)
    left_grad, left_hess = left[:4], left[4:]
    total_grad, total_hess = total[:4], total[4:]
    right_grad = total_grad - left_grad
    value = left_grad * left_grad / (left_hess + reg_lambda)
    value = value + right_grad * right_grad / (total_hess - left_hess + reg_lambda)
    value = value - total_grad * total_grad / (total_hess + reg_lambda)
    lane = lane[:4]
    bottom = jnp.float32(-jnp.inf)
    inner = lane % BINS < BINS - 1
    one = jnp.max(jnp.where(inner & (lane < BINS), value, bottom), axis=1, keepdims=True)
    two = jnp.max(jnp.where(inner & (lane >= BINS), value, bottom), axis=1, keepdims=True)
    return one, two


def gains(pieces, listeners):
    vmem = pl.BlockSpec(memory_space=pltpu.VMEM)
    return pl.pallas_call(
        gain_kernel,
        out_shape=(
            jax.ShapeDtypeStruct((4, 2), jnp.float32),
            jax.ShapeDtypeStruct((listeners, LANES), jnp.float32),
        ),
        in_specs=[vmem],
        out_specs=(vmem, vmem),
        compiler_params=pltpu.CompilerParams(vmem_limit_bytes=4 * 2**20),
        name="gains",
    )(pieces)


def body(bin_index, gradient, hessian, child_id, smaller_side):
    ny, nc, nx, nh, nm, np_ = (lax.axis_size(a) for a in AXES)
    keep, send = histograms(bin_index, gradient, hessian, child_id, smaller_side)
    chip = keep + lax.ppermute(send, "core", [(0, 1), (1, 0)])
    chip = chip.reshape(ny * nx * np_, nm * nh, 8, LANES)
    near = jnp.sum(lax.all_to_all(chip, ("y", "x", "zp"), 0, 0, tiled=True), axis=0)
    near = jnp.broadcast_to(near.reshape(nm, 1, nh, 8, LANES), (nm, nh, nh, 8, LANES))
    pieces = lax.all_to_all(near.reshape(nm * nh, nh, 8, LANES), ("zm", "zh"), 0, 0, tiled=True)
    best_gain, told = gains(pieces, nx * nm * np_)
    heard = lax.all_to_all(told, ("x", "zm", "zp"), 0, 0, tiled=True)
    child_best = jnp.max(heard, axis=0)[:4]
    return best_gain, child_best


def solution(mesh):
    split = Mesh(mesh.devices.reshape(4, 2, 4, *Z_PARTS), AXES)
    every = P(AXES)
    return jax.shard_map(
        body,
        mesh=split,
        in_specs=(P(AXES, None), every, every, every, P()),
        out_specs=(P(("y", "core"), ("x", "zh", "zm", "zp")), P(("y", "core"))),
        check_vma=False,
    )
```
